512 devices in a mesh: dp: 32 (over y_hi, x, core), ctx: 16 (over z, y_lo).
Axes of the slice: x: 4, y: 8 (y_hi: 4, y_lo: 2; y = y_hi * 2 + y_lo), z: 8, core: 2. Of those that a mesh axis runs over, the one named last changes fastest.
Arguments:
- query: bfloat16 [32, 2048, 4096], P('dp', 'ctx'), may hold values from -6 to 6
- grad_out: bfloat16 [32, 2048, 4096], P('dp', 'ctx'), may hold values from -0.75 to 0.75
- keys: bfloat16 [32, 2048, 512], P('dp', 'ctx'), may hold values from -6 to 6
- values: bfloat16 [32, 2048, 512], P('dp', 'ctx'), may hold values from -6 to 6
- log_norm: float32 [32, 2048, 32], P('dp', 'ctx'), may hold values from 4 to 8
- row_dots: float32 [32, 2048, 32], P('dp', 'ctx'), may hold values from -6 to 6
- block_input: bfloat16 [32, 2048, 4096], P('dp', 'ctx'), may hold values from -6 to 6
- route_index: int32 [32, 2048], P('dp', 'ctx'), may hold values from 0 to 1023, as said below
- counts: int32 [32, 16], P('dp', 'ctx'), may hold values from 32 to 128, as said below
Outputs:
- key_weight_grad: float32 [4096, 512], P('ctx', 'dp')
The draws below stay inside these ranges and needn't reach their ends.
Inputs may be any that keep to these rules, and one draw needn't show every extreme that they name: `route_index`: within each shard of 128 slots, the first counts slots hold distinct token indices in increasing order; the remaining slots hold 0 and are padding. `counts`: in every sequence one shard is full (128) and another holds 32.
All inputs are finite; a program needn't handle non-finite values.
Results may differ from the reference program's by a relative error of at most 0.004.
Values may be sent and summed in bfloat16 or wider, within the bound.
No kernel may reach another device: no remote copies, remote signals or barrier semaphores. Data moves between devices by JAX's collectives and lax.ppermute only.
A program may use at most 64 MiB of HBM per device.

```python
import jax
import jax.numpy as jnp
from jax import lax

HQ = 32
KVH = 4
DH = 128
D = 4096
CAP = 128
TOK_DEV = 1024
SEQS = 32
ROWS = 2048


def routed_counts(key):
    shards = ROWS // CAP
    amounts = jax.random.randint(jax.random.fold_in(key, 101), (SEQS, shards), CAP // 4, CAP + 1)
    full_at = jax.random.randint(jax.random.fold_in(key, 102), (SEQS, 1), 0, shards)
    lane = jnp.arange(shards)[None, :]
    amounts = jnp.where(lane == full_at, CAP, amounts)
    amounts = jnp.where(lane == (full_at + 1) % shards, CAP // 4, amounts)
    return amounts.astype(jnp.int32)


def draw_counts(key, part):
    return routed_counts(key)


def draw_route_index(key, part):
    amounts = routed_counts(key)
    key = jax.random.fold_in(key, 3)
    shards = ROWS // CAP
    subkeys = jax.random.split(key, SEQS * shards)
    chosen = jax.vmap(lambda single: jax.random.permutation(single, TOK_DEV)[:CAP])(subkeys)
    chosen = chosen.reshape(SEQS, shards, CAP)
    lane = jnp.arange(CAP)[None, None, :]
    marked = jnp.where(lane < amounts[:, :, None], chosen, TOK_DEV)
    ordered = jnp.sort(marked, axis=-1)
    ordered = jnp.where(ordered == TOK_DEV, 0, ordered)
    return ordered.reshape(SEQS, ROWS).astype(jnp.int32)


def block_levels(key, shape, cuts, least, top_value):
    loudness, own = 1.0, jax.random.fold_in(key, 6)
    for dim, shards_of in cuts:
        heights = jnp.exp(jax.random.uniform(jax.random.fold_in(own, dim), (shards_of,), jnp.float32, least / len(cuts), top_value / len(cuts)))
        loudness = loudness * jnp.repeat(heights, shape[dim] // shards_of).reshape([-1 if axis == dim else 1 for axis in range(len(shape))])
    return loudness


def centred(own_key, extent, scale, limit, cuts=(), kind=jnp.bfloat16):
    entries = jax.random.normal(own_key, extent, jnp.float32) * scale
    if len(cuts) > 0:
        entries = block_levels(own_key, extent, cuts, -0.22, 0.18) * entries
    return jnp.clip(entries, min=-limit, max=limit).astype(kind)


def setup_inputs(seed: int = 0) -> dict:
    seeds = jax.random.split(jax.random.key(seed), 10)
    return {
        "query": centred(seeds[0], (SEQS, ROWS, HQ * DH), 1.0, 6.0, ((0, 32), (1, 16))),
        "grad_out": centred(seeds[1], (SEQS, ROWS, HQ * DH), 0.05, 0.75, ((0, 32), (1, 16))),
        "keys": centred(seeds[2], (SEQS, ROWS, KVH * DH), 1.0, 6.0, ((0, 32), (1, 16))),
        "values": centred(seeds[3], (SEQS, ROWS, KVH * DH), 1.0, 6.0, ((0, 32), (1, 16))),
        "log_norm": jnp.clip(4.0 + 4.0 * jax.random.uniform(seeds[4], (SEQS, ROWS, HQ), jnp.float32) ** block_levels(seeds[4], (SEQS, ROWS, HQ), ((0, 32), (1, 16)), -0.2, 0.2), 4.0, 8.0),
        "row_dots": centred(seeds[5], (SEQS, ROWS, HQ), 0.5, 6.0, ((0, 32), (1, 16)), jnp.float32),
        "block_input": centred(seeds[6], (SEQS, ROWS, D), 1.0, 6.0, ((0, 32), (1, 16))),
        "route_index": draw_route_index(jax.random.fold_in(seeds[9], 71), 0),
        "counts": draw_counts(jax.random.fold_in(seeds[9], 71), 0),
    }


far_slot = 1073741824


def head_terms(q_rows, d_rows, norms, dots, q_pos, k_rows, v_rows, k_pos):
    count = q_rows.shape[0]
    number = k_rows.shape[0]
    group = HQ // KVH
    scale = DH ** -0.5
    query_heads = q_rows.astype(jnp.float32).reshape(count, KVH, group, DH)
    grad_heads = d_rows.astype(jnp.float32).reshape(count, KVH, group, DH)
    key_heads = k_rows.astype(jnp.float32).reshape(number, KVH, DH)
    value_heads = v_rows.astype(jnp.float32).reshape(number, KVH, DH)
    scores = jnp.einsum("rgie,tge->girt", query_heads, key_heads) * scale
    norm_cols = jnp.transpose(norms.reshape(count, KVH, group), (1, 2, 0))[..., None]
    dot_cols = jnp.transpose(dots.reshape(count, KVH, group), (1, 2, 0))[..., None]
    allowed = k_pos[None, :] <= q_pos[:, None]
    probs = jnp.where(allowed, jnp.exp(scores - norm_cols), 0.0)
    dprobs = jnp.einsum("rgie,tge->girt", grad_heads, value_heads)
    dscores = (probs * (dprobs - dot_cols)).astype(jnp.bfloat16)
    terms = jnp.einsum("girt,rgie->tge", dscores.astype(jnp.float32), query_heads)
    return terms.reshape(number, KVH * DH)


def reference(query, grad_out, keys, values, log_norm, row_dots, block_input, route_index, counts):
    scale = DH ** -0.5
    slot_ids = jnp.arange(ROWS, dtype=jnp.int32)
    owner = (slot_ids // CAP).astype(jnp.int32)

    def one_sequence(carry, items):
        q_seq, d_seq, k_seq, v_seq, n_seq, t_seq, x_seq, r_seq, c_seq = items
        is_valid = (slot_ids % CAP) < c_seq[owner]
        position = (owner * TOK_DEV + r_seq).astype(jnp.int32)
        key_pos = jnp.where(is_valid, position, jnp.int32(far_slot)).astype(jnp.int32)
        query_pos = jnp.where(is_valid, position, jnp.int32(-1)).astype(jnp.int32)

        def one_block(total, block):
            begin = (block * CAP).astype(jnp.int32)
            term = head_terms(
                lax.dynamic_slice_in_dim(q_seq, begin, CAP, 0),
                lax.dynamic_slice_in_dim(d_seq, begin, CAP, 0),
                lax.dynamic_slice_in_dim(n_seq, begin, CAP, 0),
                lax.dynamic_slice_in_dim(t_seq, begin, CAP, 0),
                lax.dynamic_slice_in_dim(query_pos, begin, CAP, 0),
                k_seq, v_seq, key_pos)
            return total + term, None

        start_grads = jnp.zeros((ROWS, KVH * DH), jnp.float32)
        grads, _ = lax.scan(one_block, start_grads, jnp.arange(ROWS // CAP, dtype=jnp.int32))
        key_grad = (grads * scale).astype(jnp.bfloat16)
        return carry + jnp.dot(x_seq.T, key_grad, preferred_element_type=jnp.float32), None

    start = jnp.zeros((D, KVH * DH), jnp.float32)
    result, _ = lax.scan(one_sequence, start, (query, grad_out, keys, values, log_norm, row_dots, block_input, route_index, counts))
    return result
```

```python
import functools

import jax
import jax.numpy as jnp
import numpy as np
from jax import lax
from jax.experimental import pallas as pl
from jax.experimental.pallas import tpu as pltpu
from jax.sharding import Mesh, PartitionSpec as P

HQ = 32
KVH = 4
DH = 128
GROUP = HQ // KVH
CAP = 128
D = 4096
LOG2E = 1.4426950408889634
SCALE = DH ** (-0.5)
HOME = ("zl", "yl")
HALF = GROUP // 2
CHUNK_ROWS = 2 * HALF * CAP + 32
SUPER = 4 * CAP
VMEM = 50 * 1024 * 1024


def split3(x):
    hi = x.astype(jnp.bfloat16)
    rest = x - hi.astype(jnp.float32)
    mid = rest.astype(jnp.bfloat16)
    lo = (rest - mid.astype(jnp.float32)).astype(jnp.bfloat16)
    return hi, mid, lo


def whole(*shape):
    return pl.BlockSpec(memory_space=pltpu.VMEM)


def pack_kv_kernel(count_ref, k_ref, v_ref, out_ref):
    rows = lax.broadcasted_iota(jnp.int32, (CAP, DH), 0)
    valid = rows < count_ref[0, 0]
    for g in range(KVH):
        cols = slice(g * DH, (g + 1) * DH)
        out_ref[g, 0] = jnp.where(valid, k_ref[:, cols], jnp.zeros((), jnp.bfloat16))
        out_ref[g, 1] = v_ref[:, cols]


def pack_kv(counts, keys, values):
    return pl.pallas_call(
        pack_kv_kernel,
        out_shape=jax.ShapeDtypeStruct((KVH, 2, CAP, DH), jnp.bfloat16),
        in_specs=[pl.BlockSpec(memory_space=pltpu.SMEM), whole(), whole()],
        out_specs=whole(),
        compiler_params=pltpu.CompilerParams(vmem_limit_bytes=VMEM),
        name="pack_kv",
    )(counts, keys, values)


def pack_q_kernel(chunk, count_ref, q_ref, d_ref, n_ref, t_ref, out_ref):
    g = pl.program_id(0)
    for h in range(HALF):
        cols = slice(h * DH, (h + 1) * DH)
        out_ref[0, h * CAP:(h + 1) * CAP] = q_ref[:, cols]
        out_ref[0, (HALF + h) * CAP:(HALF + h + 1) * CAP] = d_ref[:, cols]
    lane = lax.broadcasted_iota(jnp.int32, (HQ, CAP), 1)
    norms = jnp.where(lane < count_ref[0, 0], n_ref[...] * LOG2E, jnp.float32(1e30))
    dots = t_ref[...]
    base = 2 * HALF * CAP
    for which in range(KVH):

        @pl.when(g == which)
        def _():
            heads = slice(which * GROUP + chunk * HALF, which * GROUP + (chunk + 1) * HALF)
            parts = [*split3(norms[heads]), *split3(dots[heads])]
            parts.append(jnp.zeros((8, CAP), jnp.bfloat16))
            out_ref[0, base:base + 32] = jnp.concatenate(
                [p.astype(jnp.float32) for p in parts], axis=0
            ).astype(jnp.bfloat16)


def pack_q(chunk, counts, query, grad, norms_t, dots_t):
    part = lambda g: (0, 2 * g + chunk)
    return pl.pallas_call(
        functools.partial(pack_q_kernel, chunk),
        grid=(KVH,),
        out_shape=jax.ShapeDtypeStruct((KVH, CHUNK_ROWS, DH), jnp.bfloat16),
        in_specs=[
            pl.BlockSpec(memory_space=pltpu.SMEM),
            pl.BlockSpec((CAP, HALF * DH), part),
            pl.BlockSpec((CAP, HALF * DH), part),
            pl.BlockSpec((HQ, CAP), lambda g: (0, 0)),
            pl.BlockSpec((HQ, CAP), lambda g: (0, 0)),
        ],
        out_specs=pl.BlockSpec((1, CHUNK_ROWS, DH), lambda g: (g, 0, 0)),
        compiler_params=pltpu.CompilerParams(vmem_limit_bytes=VMEM),
        name="pack_q%d" % chunk,
    )(counts, query, grad, norms_t, dots_t)


def pack_x_kernel(count_ref, x_ref, out_ref):
    rows = lax.broadcasted_iota(jnp.int32, (CAP, 256), 0)
    valid = rows < count_ref[0, 0]
    for z in range(4):
        for j in range(4):
            begin = z * 1024 + j * 256
            out_ref[j, :, z * 256:(z + 1) * 256] = jnp.where(
                valid, x_ref[:, begin:begin + 256], jnp.zeros((), jnp.bfloat16)
            )


def pack_x(counts, x):
    return pl.pallas_call(
        pack_x_kernel,
        out_shape=jax.ShapeDtypeStruct((4, CAP, 1024), jnp.bfloat16),
        in_specs=[pl.BlockSpec(memory_space=pltpu.SMEM), whole()],
        out_specs=whole(),
        compiler_params=pltpu.CompilerParams(vmem_limit_bytes=VMEM),
        name="pack_x",
    )(counts, x)


NT = (((1,), (1,)), ((), ()))
NN = (((1,), (0,)), ((), ()))


def rows_of(qd_ref, j):
    base = 2 * HALF * CAP
    small = qd_ref[j, base:base + 32].astype(jnp.float32)
    norm = small[0:4] + small[4:8] + small[8:12]
    dot = small[12:16] + small[16:20] + small[20:24]
    return norm, dot


def dscores(scores, dprobs, norm, dot, keep=None):
    out = []
    for h in range(HALF):
        cols = slice(h * CAP, (h + 1) * CAP)
        p = jnp.exp2(scores[:, cols] * (SCALE * LOG2E) - norm[h:h + 1])
        if keep is not None:
            p = jnp.where(keep, p, 0.0)
        out.append((p * (dprobs[:, cols] - dot[h:h + 1])).astype(jnp.bfloat16))
    return jnp.concatenate(out, axis=1)


def attend(qd_ref, j, k, v, rows=None, keep=None):
    q = qd_ref[j, 0:HALF * CAP]
    d = qd_ref[j, HALF * CAP:2 * HALF * CAP]
    norm, dot = rows
    scores = lax.dot_general(k, q, NT, preferred_element_type=jnp.float32)
    dprobs = lax.dot_general(v, d, NT, preferred_element_type=jnp.float32)
    ds = dscores(scores, dprobs, norm, dot, keep)
    return lax.dot_general(ds, q, NN, preferred_element_type=jnp.float32)


def attend_kernel(first, place_ref, qd_ref, own_ref, r1_ref, l1_ref, ra_ref, lb_ref, *rest):
    if first:
        (out_ref,) = rest
    else:
        before_ref, out_ref = rest
    zh = place_ref[0]

    def far(dist, kv):
        at = lax.rem(zh - dist + 4, 4)

        @pl.when(zh >= dist)
        def _():
            def step(j, _):
                k, v = kv()
                term = attend(qd_ref, j, k, v, rows_of(qd_ref, j))

                @pl.when(j == 0)
                def _():
                    acc_ref = out_ref if first else before_ref
                    if first:
                        out_ref[at] = term
                    else:
                        out_ref[at] = (acc_ref[at] + term).astype(out_ref.dtype)

                @pl.when(j > 0)
                def _():
                    out_ref[at] = (out_ref[at] + term).astype(out_ref.dtype)

                return 0

            lax.fori_loop(0, 4, step, 0)

        @pl.when(zh < dist)
        def _():
            out_ref[at] = jnp.zeros((SUPER, DH), out_ref.dtype)

    def stack(ref, which):
        return ref[:, which].reshape(-1, DH)

    row = lax.broadcasted_iota(jnp.int32, (CAP, CAP), 0)
    lane = lax.broadcasted_iota(jnp.int32, (CAP, CAP), 1)
    out_ref[zh] = jnp.zeros((SUPER, DH), out_ref.dtype) if first else before_ref[zh]
    for j in range(4):
        small = rows_of(qd_ref, j)
        term = attend(qd_ref, j, own_ref[j, 0], own_ref[j, 1], small, row <= lane)
        out_ref[zh, j * CAP:(j + 1) * CAP] += term
        if j > 0:
            k = own_ref[0:j, 0].reshape(j * CAP, DH)
            v = own_ref[0:j, 1].reshape(j * CAP, DH)
            out_ref[zh, 0:j * CAP] += attend(qd_ref, j, k, v, small)
    far(1, lambda: (stack(r1_ref, 0), stack(r1_ref, 1)))
    far(3, lambda: (stack(l1_ref, 0), stack(l1_ref, 1)))
    far(
        2,
        lambda: tuple(
            jnp.concatenate([stack(ra_ref, i), stack(lb_ref, i)], axis=0) for i in range(2)
        ),
    )


def attend_call(place, qd, blocks, before=None):
    first = before is None
    args = [place, qd, *blocks] + ([] if first else [before])
    return pl.pallas_call(
        functools.partial(attend_kernel, first),
        out_shape=jax.ShapeDtypeStruct((4, SUPER, DH), jnp.float32),
        in_specs=[pl.BlockSpec(memory_space=pltpu.SMEM)] + [whole()] * (len(args) - 1),
        out_specs=whole(),
        compiler_params=pltpu.CompilerParams(vmem_limit_bytes=VMEM),
        name="attend_first" if first else "attend_next",
    )(*args)


def key_grad_kernel(part_ref, out_ref):
    total = part_ref[0].astype(jnp.float32)
    for z in range(1, 4):
        total = total + part_ref[z].astype(jnp.float32)
    grad = (total * SCALE).T.astype(jnp.bfloat16)
    for core in range(2):
        piece = jnp.concatenate(
            [grad[x * 32 + core * 16:x * 32 + core * 16 + 16] for x in range(4)], axis=0
        )
        for j in range(4):
            out_ref[core, j] = piece


def key_grad_call(parts):
    return pl.pallas_call(
        key_grad_kernel,
        out_shape=jax.ShapeDtypeStruct((2, 4, 64, SUPER), jnp.bfloat16),
        in_specs=[whole()],
        out_specs=whole(),
        compiler_params=pltpu.CompilerParams(vmem_limit_bytes=VMEM),
        name="key_grad",
    )(parts)


def project_kernel(core_ref, grad_ref, mine_ref, other_ref, out_ref):
    core = core_ref[0]
    mine = grad_ref[core].reshape(256, SUPER)
    other = grad_ref[1 - core].reshape(256, SUPER)
    total = lax.dot_general(
        mine, mine_ref[...].reshape(SUPER, 1024), NN, preferred_element_type=jnp.float32
    ) + lax.dot_general(
        other, other_ref[...].reshape(SUPER, 1024), NN, preferred_element_type=jnp.float32
    )
    total = total.astype(jnp.bfloat16)
    for c in range(16):
        for z in range(4):
            out_ref[c, z] = total[c * 16:(c + 1) * 16, z * 256:(z + 1) * 256]


def project(core, grads, mine, other):
    return pl.pallas_call(
        project_kernel,
        out_shape=jax.ShapeDtypeStruct((16, 4, 16, 256), jnp.bfloat16),
        in_specs=[pl.BlockSpec(memory_space=pltpu.SMEM)] + [whole()] * 3,
        out_specs=whole(),
        compiler_params=pltpu.CompilerParams(vmem_limit_bytes=VMEM),
        name="project",
    )(core, grads, mine, other)


def total_kernel(part_ref, out_ref):
    def step(i, total):
        return total + part_ref[i].astype(jnp.float32)

    total = part_ref[0].astype(jnp.float32)
    for i in range(1, 64):
        total = step(i, total)
    out_ref[...] = total.T


def total_call(parts):
    return pl.pallas_call(
        total_kernel,
        out_shape=jax.ShapeDtypeStruct((256, 16), jnp.float32),
        in_specs=[whole()],
        out_specs=whole(),
        compiler_params=pltpu.CompilerParams(vmem_limit_bytes=VMEM),
        name="total",
    )(parts)


def shift(x, step):
    return lax.ppermute(x, "zh", [(i, (i + step) % 4) for i in range(4)])


def body(query, grad_out, keys, values, log_norm, row_dots, block_input, route_index, counts):
    del route_index
    place = lax.axis_index("zh").reshape(1).astype(jnp.int32)
    core = lax.axis_index("core").reshape(1).astype(jnp.int32)
    kv = pack_kv(counts, keys[0], values[0])
    own = lax.all_to_all(kv, HOME, 0, 0)
    norms_t, dots_t = log_norm[0].T, row_dots[0].T
    queries = [
        lax.all_to_all(pack_q(c, counts, query[0], grad_out[0], norms_t, dots_t), HOME, 0, 0)
        for c in range(2)
    ]
    r1, l1 = shift(own, 1), shift(own, -1)
    ra, lb = shift(r1[:2], 1), shift(l1[2:], -1)
    mine = lax.all_to_all(pack_x(counts, block_input[0]), HOME, 0, 0)
    other = lax.ppermute(mine, "core", [(0, 1), (1, 0)])
    blocks = (own, r1, l1, ra, lb)
    terms = attend_call(place, queries[0], blocks)
    terms = attend_call(place, queries[1], blocks, terms)
    parts = lax.all_to_all(terms.astype(jnp.bfloat16), "zh", 0, 0)
    grads = key_grad_call(parts)
    grads = lax.all_to_all(grads.reshape(8, 64, SUPER), ("core",) + HOME, 0, 0)
    local = project(core, grads.reshape(2, 4, 64, SUPER), mine, other)
    pieces = lax.all_to_all(local.reshape(64, 16, 256), ("yh", "x", "zh"), 0, 0)
    return total_call(pieces)


def solution(mesh):
    fine = Mesh(
        np.asarray(mesh.devices).reshape(4, 4, 2, 4, 2, 2), ("yh", "x", "core", "zh", "zl", "yl")
    )
    dp, ctx = ("yh", "x", "core"), ("zh", "zl", "yl")
    in_specs = (P(dp, ctx, None),) * 7 + (P(dp, ctx),) * 2
    return jax.shard_map(body, mesh=fine, in_specs=in_specs, out_specs=P(ctx, dp), check_vma=False)
```

```python
import functools

import jax
import jax.numpy as jnp
import numpy as np
from jax import lax
from jax.experimental import pallas as pl
from jax.experimental.pallas import tpu as pltpu
from jax.sharding import Mesh, PartitionSpec as P

HQ = 32
KVH = 4
DH = 128
GROUP = HQ // KVH
CAP = 128
D = 4096
LOG2E = 1.4426950408889634
SCALE = DH ** (-0.5)
HOME = ("zl", "yl")
HALF = GROUP // 2
PACK_ROWS = 2 * GROUP * CAP + 8 * GROUP
SUPER = 4 * CAP
VMEM = 24 * 1024 * 1024
MOST_VMEM = 60 * 1024 * 1024


def split3(x):
    hi = x.astype(jnp.bfloat16)
    rest = x - hi.astype(jnp.float32)
    mid = rest.astype(jnp.bfloat16)
    lo = (rest - mid.astype(jnp.float32)).astype(jnp.bfloat16)
    return hi, mid, lo


def whole(*shape):
    return pl.BlockSpec(memory_space=pltpu.VMEM)


def pack_kv_kernel(count_ref, k_ref, v_ref, out_ref):
    rows = lax.broadcasted_iota(jnp.int32, (CAP, DH), 0)
    valid = rows < count_ref[0, 0]
    for g in range(KVH):
        cols = slice(g * DH, (g + 1) * DH)
        k = jnp.where(valid, k_ref[:, cols], jnp.zeros((), jnp.bfloat16))
        v = v_ref[:, cols]
        for z in range(4):
            out_ref[z, g, 0] = k
            out_ref[z, g, 1] = v


def pack_kv(counts, keys, values):
    return pl.pallas_call(
        pack_kv_kernel,
        out_shape=jax.ShapeDtypeStruct((4, KVH, 2, CAP, DH), jnp.bfloat16),
        in_specs=[pl.BlockSpec(memory_space=pltpu.SMEM), whole(), whole()],
        out_specs=whole(),
        compiler_params=pltpu.CompilerParams(vmem_limit_bytes=MOST_VMEM),
        name="pack_kv",
    )(counts, keys, values)


def pack_q_kernel(head_ref, count_ref, q_ref, d_ref, n_ref, t_ref, out_ref):
    for h in range(GROUP):
        cols = slice(h * DH, (h + 1) * DH)
        out_ref[h * CAP:(h + 1) * CAP] = q_ref[:, cols]
        out_ref[(GROUP + h) * CAP:(GROUP + h + 1) * CAP] = d_ref[:, cols]
    lane = lax.broadcasted_iota(jnp.int32, (GROUP, CAP), 1)
    norms = jnp.where(lane < count_ref[0], n_ref[...] * LOG2E, jnp.float32(1e30))
    parts = [*split3(norms), *split3(t_ref[...])]
    parts += [jnp.zeros((GROUP, CAP), jnp.bfloat16)] * 2
    out_ref[2 * GROUP * CAP:] = jnp.concatenate(
        [p.astype(jnp.float32) for p in parts], axis=0
    ).astype(jnp.bfloat16)


def pack_q(head, counts, query, grad, norms_t, dots_t):
    cols = lambda i, head, count: (0, head[0])
    rows = lambda i, head, count: (head[0], 0)
    return pl.pallas_call(
        pack_q_kernel,
        grid_spec=pltpu.PrefetchScalarGridSpec(
            num_scalar_prefetch=2,
            grid=(1,),
            in_specs=[
                pl.BlockSpec((CAP, GROUP * DH), cols),
                pl.BlockSpec((CAP, GROUP * DH), cols),
                pl.BlockSpec((GROUP, CAP), rows),
                pl.BlockSpec((GROUP, CAP), rows),
            ],
            out_specs=pl.BlockSpec((PACK_ROWS, DH), lambda i, head, count: (0, 0)),
        ),
        out_shape=jax.ShapeDtypeStruct((PACK_ROWS, DH), jnp.bfloat16),
        compiler_params=pltpu.CompilerParams(vmem_limit_bytes=VMEM),
        name="pack_q",
    )(head, counts.reshape(1), query, grad, norms_t, dots_t)


def pack_x_kernel(home_ref, count_ref, x_ref, *out_refs):
    rows = lax.broadcasted_iota(jnp.int32, (CAP, 256), 0)
    valid = rows < count_ref[0, 0]
    for flip, out_ref in enumerate(out_refs):
        for z in range(4):
            begin = pl.multiple_of(z * 1024 + (home_ref[0] ^ flip) * 256, 256)
            out_ref[:, z * 256:(z + 1) * 256] = jnp.where(
                valid, x_ref[:, pl.ds(begin, 256)], jnp.zeros((), jnp.bfloat16)
            )


def pack_x(home, counts, x):
    return pl.pallas_call(
        pack_x_kernel,
        out_shape=[jax.ShapeDtypeStruct((CAP, D // 4), jnp.bfloat16)] * 4,
        in_specs=[pl.BlockSpec(memory_space=pltpu.SMEM)] * 2 + [whole()],
        out_specs=[whole()] * 4,
        compiler_params=pltpu.CompilerParams(vmem_limit_bytes=VMEM),
        name="pack_x",
    )(home, counts, x)


def join_x_kernel(home_ref, *refs):
    for flip, ref in enumerate(refs[:-1]):
        refs[-1][home_ref[0] ^ flip] = ref[...]


def join_x(home, parts):
    return pl.pallas_call(
        join_x_kernel,
        out_shape=jax.ShapeDtypeStruct((4, CAP, D // 4), jnp.bfloat16),
        in_specs=[pl.BlockSpec(memory_space=pltpu.SMEM)] + [whole()] * 4,
        out_specs=whole(),
        compiler_params=pltpu.CompilerParams(vmem_limit_bytes=VMEM),
        name="join_x",
    )(home, *parts)


NT = (((1,), (1,)), ((), ()))
NN = (((1,), (0,)), ((), ()))


def attend(qd_ref, k, v, keep=None):
    q = qd_ref[0:GROUP * CAP]
    d = qd_ref[GROUP * CAP:2 * GROUP * CAP]
    small = qd_ref[2 * GROUP * CAP:].astype(jnp.float32)
    norm = small[0:8] + small[8:16] + small[16:24]
    dot = small[24:32] + small[32:40] + small[40:48]
    out = []
    for half in range(2):
        part = slice(half * HALF * CAP, (half + 1) * HALF * CAP)
        scores = lax.dot_general(k, q[part], NT, preferred_element_type=jnp.float32)
        dprobs = lax.dot_general(v, d[part], NT, preferred_element_type=jnp.float32)
        for i in range(HALF):
            cols = slice(i * CAP, (i + 1) * CAP)
            h = half * HALF + i
            p = jnp.exp2(scores[:, cols] * (SCALE * LOG2E) - norm[h:h + 1])
            if keep is not None:
                p = jnp.where(keep, p, 0.0)
            out.append((p * (dprobs[:, cols] - dot[h:h + 1])).astype(jnp.bfloat16))
    ds = jnp.concatenate(out, axis=1)
    return lax.dot_general(ds, q, NN, preferred_element_type=jnp.float32)


def far_kernel(count, place_ref, kv_ref, *rest):
    q_refs, out_ref = rest[:count], rest[-1]
    zh = place_ref[0]

    def earlier(at, carry):
        keys = pl.ds(4 * at, 4)
        k = kv_ref[keys, 0].reshape(SUPER, DH)
        v = kv_ref[keys, 1].reshape(SUPER, DH)
        for i, q_ref in enumerate(q_refs):
            term = attend(q_ref, k, v)
            if i > 0:
                term = term + out_ref[at]
            elif len(rest) > count + 1:
                term = term + rest[count][at]
            out_ref[at] = term.astype(out_ref.dtype)
        return carry

    def later(at, carry):
        out_ref[at] = jnp.zeros((SUPER, DH), out_ref.dtype)
        return carry

    lax.fori_loop(0, zh, earlier, 0)
    lax.fori_loop(zh, 4, later, 0)


def far_call(place, kv, queries, before=None, kind=jnp.float32):
    args = [place, kv, *queries] + ([] if before is None else [before])
    return pl.pallas_call(
        functools.partial(far_kernel, len(queries)),
        out_shape=jax.ShapeDtypeStruct((4, SUPER, DH), kind),
        in_specs=[pl.BlockSpec(memory_space=pltpu.SMEM)] + [whole()] * (len(args) - 1),
        out_specs=whole(),
        compiler_params=pltpu.CompilerParams(vmem_limit_bytes=VMEM),
        cost_estimate=pl.CostEstimate(flops=1, bytes_accessed=1, transcendentals=0),
        name="far_%d" % len(queries),
    )(*args)


def near_kernel(flips, place_ref, kv_ref, *rest):
    q_refs, out_ref = rest[:len(flips)], rest[-1]
    keys = pl.ds(4 * place_ref[0], 4)
    k = kv_ref[keys, 0].reshape(SUPER, DH)
    v = kv_ref[keys, 1].reshape(SUPER, DH)
    row = lax.broadcasted_iota(jnp.int32, (SUPER, CAP), 0)
    lane = lax.broadcasted_iota(jnp.int32, (SUPER, CAP), 1)
    for i, (flip, q_ref) in enumerate(zip(flips, q_refs)):
        term = attend(q_ref, k, v, row <= lane + CAP * (place_ref[1] ^ flip))
        if i > 0:
            term = term + out_ref[...]
        elif len(rest) > len(flips) + 1:
            term = term + rest[-2][...]
        out_ref[...] = term


def near_call(place, kv, flips, queries, before=None):
    args = [place, kv, *queries] + ([] if before is None else [before])
    return pl.pallas_call(
        functools.partial(near_kernel, flips),
        out_shape=jax.ShapeDtypeStruct((SUPER, DH), jnp.float32),
        in_specs=[pl.BlockSpec(memory_space=pltpu.SMEM)] + [whole()] * (len(args) - 1),
        out_specs=whole(),
        compiler_params=pltpu.CompilerParams(vmem_limit_bytes=VMEM),
        cost_estimate=pl.CostEstimate(flops=1, bytes_accessed=1, transcendentals=0),
        name="near_%d" % flips[0],
    )(*args)


def key_grad_kernel(part_ref, near_ref, out_ref):
    total = near_ref[...]
    for z in range(4):
        total = total + part_ref[z].astype(jnp.float32)
    grad = (total * SCALE).T.astype(jnp.bfloat16)
    for core in range(2):
        rows = [x * 32 + core * 16 for x in range(4)]
        piece = jnp.concatenate([grad[r:r + 16] for r in rows], axis=0)
        for j in range(4):
            out_ref[core, j] = piece


def key_grad_call(parts, near):
    return pl.pallas_call(
        key_grad_kernel,
        out_shape=jax.ShapeDtypeStruct((2, 4, 64, SUPER), jnp.bfloat16),
        in_specs=[whole()] * 2,
        out_specs=whole(),
        compiler_params=pltpu.CompilerParams(vmem_limit_bytes=VMEM),
        name="key_grad",
    )(parts, near)


def project_kernel(core_ref, grad_ref, *refs):
    out_ref = refs[-1]
    total = None
    for flip, x_ref in enumerate(refs[:-1]):
        grad = grad_ref[core_ref[0] ^ flip].reshape(256, SUPER)
        x = x_ref[...].reshape(SUPER, D // 4)
        term = lax.dot_general(grad, x, NN, preferred_element_type=jnp.float32)
        total = term if total is None else total + term
    total = total.astype(jnp.bfloat16)
    for c in range(16):
        for z in range(4):
            out_ref[c, z] = total[c * 16:(c + 1) * 16, z * 256:(z + 1) * 256]


def project(core, grads, features):
    return pl.pallas_call(
        project_kernel,
        out_shape=jax.ShapeDtypeStruct((16, 4, 16, 256), jnp.bfloat16),
        in_specs=[pl.BlockSpec(memory_space=pltpu.SMEM)] + [whole()] * 3,
        out_specs=whole(),
        compiler_params=pltpu.CompilerParams(vmem_limit_bytes=VMEM),
        name="project",
    )(core, grads, *features)


def total_kernel(part_ref, out_ref):
    def step(i, total):
        return total + part_ref[i].astype(jnp.float32)

    total = part_ref[0].astype(jnp.float32)
    for i in range(1, 64):
        total = step(i, total)
    out_ref[...] = total.T


def total_call(parts):
    return pl.pallas_call(
        total_kernel,
        out_shape=jax.ShapeDtypeStruct((256, 16), jnp.float32),
        in_specs=[whole()],
        out_specs=whole(),
        compiler_params=pltpu.CompilerParams(vmem_limit_bytes=VMEM),
        name="total",
    )(parts)


def body(query, grad_out, keys, values, log_norm, row_dots, block_input, route_index, counts):
    del route_index
    zh = lax.axis_index("zh").astype(jnp.int32)
    home = lax.axis_index(HOME).astype(jnp.int32)
    core = lax.axis_index("core").astype(jnp.int32)
    kv = pack_kv(counts, keys[0], values[0]).reshape(16, 2, CAP, DH)
    kv = lax.all_to_all(kv, ("zh",) + HOME, 0, 0)
    norms_t, dots_t = log_norm[0].T, row_dots[0].T

    def to_home(x, flip):
        if flip == 0:
            return x
        return lax.ppermute(x, HOME, [(i, i ^ flip) for i in range(4)])

    def queries(flip):
        head = (home ^ flip).reshape(1)
        return to_home(pack_q(head, counts, query[0], grad_out[0], norms_t, dots_t), flip)

    place = jnp.stack([zh, home])
    own, beside_y, beside_z, diagonal = (queries(flip) for flip in range(4))
    pieces = list(pack_x(home.reshape(1), counts, block_input[0]))
    pieces[1] = to_home(pieces[1], 1)
    kv, beside_y = lax.optimization_barrier((kv, beside_y))
    far = far_call(place, kv, [own, beside_y])
    near = near_call(place, kv, (0, 1), [own, beside_y])
    far, near, *pieces[2:] = lax.optimization_barrier((far, near, *pieces[2:]))
    pieces[2:] = to_home(pieces[2], 2), to_home(pieces[3], 3)
    far, near, beside_z, diagonal = lax.optimization_barrier((far, near, beside_z, diagonal))
    far = far_call(place, kv, [beside_z, diagonal], far, jnp.bfloat16)
    far, *pieces = lax.optimization_barrier((far, *pieces))
    parts = lax.all_to_all(far, "zh", 0, 0)
    mine = join_x(home.reshape(1), pieces)
    other = lax.ppermute(mine, "core", [(0, 1), (1, 0)])
    near = near_call(place, kv, (2, 3), [beside_z, diagonal], near)
    grads = key_grad_call(parts, near)
    grads = lax.all_to_all(grads.reshape(8, 64, SUPER), ("core",) + HOME, 0, 0)
    local = project(core.reshape(1), grads.reshape(2, 4, 64, SUPER), [mine, other])
    parts = lax.all_to_all(local.reshape(64, 16, 256), ("yh", "x", "zh"), 0, 0)
    return total_call(parts)


def solution(mesh):
    fine = Mesh(
        np.asarray(mesh.devices).reshape(4, 4, 2, 4, 2, 2), ("yh", "x", "core", "zh", "zl", "yl")
    )
    dp, ctx = ("yh", "x", "core"), ("zh", "zl", "yl")
    in_specs = (P(dp, ctx, None),) * 7 + (P(dp, ctx),) * 2
    return jax.shard_map(body, mesh=fine, in_specs=in_specs, out_specs=P(ctx, dp), check_vma=False)
```

```python
import functools

import jax
import jax.numpy as jnp
import numpy as np
from jax import lax
from jax.experimental import pallas as pl
from jax.experimental.pallas import tpu as pltpu
from jax.sharding import Mesh, PartitionSpec as P

HQ = 32
KVH = 4
DH = 128
GROUP = HQ // KVH
CAP = 128
D = 4096
LOG2E = 1.4426950408889634
SCALE = DH ** (-0.5)
HOME = ("zl", "yl")
HALF = GROUP // 2
PACK_ROWS = 2 * GROUP * CAP + 8 * GROUP
SUPER = 4 * CAP
VMEM = 24 * 1024 * 1024
MOST_VMEM = 60 * 1024 * 1024


def split3(x):
    hi = x.astype(jnp.bfloat16)
    rest = x - hi.astype(jnp.float32)
    mid = rest.astype(jnp.bfloat16)
    lo = (rest - mid.astype(jnp.float32)).astype(jnp.bfloat16)
    return hi, mid, lo


def whole(*shape):
    return pl.BlockSpec(memory_space=pltpu.VMEM)


def pack_kv_kernel(count_ref, k_ref, v_ref, out_ref):
    rows = lax.broadcasted_iota(jnp.int32, (CAP, DH), 0)
    valid = rows < count_ref[0, 0]
    for g in range(KVH):
        cols = slice(g * DH, (g + 1) * DH)
        k = jnp.where(valid, k_ref[:, cols], jnp.zeros((), jnp.bfloat16))
        v = v_ref[:, cols]
        for z in range(4):
            out_ref[z, g, 0] = k
            out_ref[z, g, 1] = v


def pack_kv(counts, keys, values):
    return pl.pallas_call(
        pack_kv_kernel,
        out_shape=jax.ShapeDtypeStruct((4, KVH, 2, CAP, DH), jnp.bfloat16),
        in_specs=[pl.BlockSpec(memory_space=pltpu.SMEM), whole(), whole()],
        out_specs=whole(),
        compiler_params=pltpu.CompilerParams(vmem_limit_bytes=MOST_VMEM),
        name="pack_kv",
    )(counts, keys, values)


def pack_q_kernel(head_ref, count_ref, q_ref, d_ref, n_ref, t_ref, out_ref):
    for h in range(GROUP):
        cols = slice(h * DH, (h + 1) * DH)
        out_ref[h * CAP:(h + 1) * CAP] = q_ref[:, cols]
        out_ref[(GROUP + h) * CAP:(GROUP + h + 1) * CAP] = d_ref[:, cols]
    lane = lax.broadcasted_iota(jnp.int32, (GROUP, CAP), 1)
    norms = jnp.where(lane < count_ref[0], n_ref[...] * LOG2E, jnp.float32(1e30))
    parts = [*split3(norms), *split3(t_ref[...])]
    parts += [jnp.zeros((GROUP, CAP), jnp.bfloat16)] * 2
    out_ref[2 * GROUP * CAP:] = jnp.concatenate(
        [p.astype(jnp.float32) for p in parts], axis=0
    ).astype(jnp.bfloat16)


def pack_q(head, counts, query, grad, norms_t, dots_t):
    cols = lambda i, head, count: (0, head[0])
    rows = lambda i, head, count: (head[0], 0)
    return pl.pallas_call(
        pack_q_kernel,
        grid_spec=pltpu.PrefetchScalarGridSpec(
            num_scalar_prefetch=2,
            grid=(1,),
            in_specs=[
                pl.BlockSpec((CAP, GROUP * DH), cols),
                pl.BlockSpec((CAP, GROUP * DH), cols),
                pl.BlockSpec((GROUP, CAP), rows),
                pl.BlockSpec((GROUP, CAP), rows),
            ],
            out_specs=pl.BlockSpec((PACK_ROWS, DH), lambda i, head, count: (0, 0)),
        ),
        out_shape=jax.ShapeDtypeStruct((PACK_ROWS, DH), jnp.bfloat16),
        compiler_params=pltpu.CompilerParams(vmem_limit_bytes=VMEM),
        name="pack_q",
    )(head, counts.reshape(1), query, grad, norms_t, dots_t)


def pack_x_kernel(home_ref, count_ref, x_ref, *out_refs):
    rows = lax.broadcasted_iota(jnp.int32, (CAP, 256), 0)
    valid = rows < count_ref[0, 0]
    for flip, out_ref in enumerate(out_refs):
        for z in range(4):
            begin = pl.multiple_of(z * 1024 + (home_ref[0] ^ flip) * 256, 256)
            out_ref[:, z * 256:(z + 1) * 256] = jnp.where(
                valid, x_ref[:, pl.ds(begin, 256)], jnp.zeros((), jnp.bfloat16)
            )


def pack_x(home, counts, x):
    return pl.pallas_call(
        pack_x_kernel,
        out_shape=[jax.ShapeDtypeStruct((CAP, D // 4), jnp.bfloat16)] * 4,
        in_specs=[pl.BlockSpec(memory_space=pltpu.SMEM)] * 2 + [whole()],
        out_specs=[whole()] * 4,
        compiler_params=pltpu.CompilerParams(vmem_limit_bytes=VMEM),
        name="pack_x",
    )(home, counts, x)


def join_x_kernel(home_ref, *refs):
    for flip, ref in enumerate(refs[:-1]):
        refs[-1][home_ref[0] ^ flip] = ref[...]


def join_x(home, parts):
    return pl.pallas_call(
        join_x_kernel,
        out_shape=jax.ShapeDtypeStruct((4, CAP, D // 4), jnp.bfloat16),
        in_specs=[pl.BlockSpec(memory_space=pltpu.SMEM)] + [whole()] * 4,
        out_specs=whole(),
        compiler_params=pltpu.CompilerParams(vmem_limit_bytes=VMEM),
        name="join_x",
    )(home, *parts)


NT = (((1,), (1,)), ((), ()))
NN = (((1,), (0,)), ((), ()))


def attend(qd_ref, k, v, keep=None):
    q = qd_ref[0:GROUP * CAP]
    d = qd_ref[GROUP * CAP:2 * GROUP * CAP]
    small = qd_ref[2 * GROUP * CAP:].astype(jnp.float32)
    norm = small[0:8] + small[8:16] + small[16:24]
    dot = small[24:32] + small[32:40] + small[40:48]
    out = []
    for half in range(2):
        part = slice(half * HALF * CAP, (half + 1) * HALF * CAP)
        scores = lax.dot_general(k, q[part], NT, preferred_element_type=jnp.float32)
        dprobs = lax.dot_general(v, d[part], NT, preferred_element_type=jnp.float32)
        for i in range(HALF):
            cols = slice(i * CAP, (i + 1) * CAP)
            h = half * HALF + i
            p = jnp.exp2(scores[:, cols] * (SCALE * LOG2E) - norm[h:h + 1])
            if keep is not None:
                p = jnp.where(keep, p, 0.0)
            out.append((p * (dprobs[:, cols] - dot[h:h + 1])).astype(jnp.bfloat16))
    ds = jnp.concatenate(out, axis=1)
    return lax.dot_general(ds, q, NN, preferred_element_type=jnp.float32)


def far_kernel(count, place_ref, kv_ref, *rest):
    q_refs, out_ref = rest[:count], rest[-1]
    zh = place_ref[0]

    def earlier(at, carry):
        keys = pl.ds(4 * at, 4)
        k = kv_ref[keys, 0].reshape(SUPER, DH)
        v = kv_ref[keys, 1].reshape(SUPER, DH)
        for i, q_ref in enumerate(q_refs):
            term = attend(q_ref, k, v)
            if i > 0:
                term = term + out_ref[at]
            elif len(rest) > count + 1:
                term = term + rest[count][at]
            out_ref[at] = term.astype(out_ref.dtype)
        return carry

    def later(at, carry):
        out_ref[at] = jnp.zeros((SUPER, DH), out_ref.dtype)
        return carry

    lax.fori_loop(0, zh, earlier, 0)
    lax.fori_loop(zh, 4, later, 0)


def far_call(place, kv, queries, before=None, kind=jnp.float32):
    args = [place, kv, *queries] + ([] if before is None else [before])
    return pl.pallas_call(
        functools.partial(far_kernel, len(queries)),
        out_shape=jax.ShapeDtypeStruct((4, SUPER, DH), kind),
        in_specs=[pl.BlockSpec(memory_space=pltpu.SMEM)] + [whole()] * (len(args) - 1),
        out_specs=whole(),
        compiler_params=pltpu.CompilerParams(vmem_limit_bytes=VMEM),
        cost_estimate=pl.CostEstimate(flops=1, bytes_accessed=1, transcendentals=0),
        name="far_%d" % len(queries),
    )(*args)


def near_kernel(flips, place_ref, kv_ref, *rest):
    q_refs, out_ref = rest[:len(flips)], rest[-1]
    keys = pl.ds(4 * place_ref[0], 4)
    k = kv_ref[keys, 0].reshape(SUPER, DH)
    v = kv_ref[keys, 1].reshape(SUPER, DH)
    row = lax.broadcasted_iota(jnp.int32, (SUPER, CAP), 0)
    lane = lax.broadcasted_iota(jnp.int32, (SUPER, CAP), 1)
    for i, (flip, q_ref) in enumerate(zip(flips, q_refs)):
        term = attend(q_ref, k, v, row <= lane + CAP * (place_ref[1] ^ flip))
        if i > 0:
            term = term + out_ref[...]
        elif len(rest) > len(flips) + 1:
            term = term + rest[-2][...]
        out_ref[...] = term


def near_call(place, kv, flips, queries, before=None):
    args = [place, kv, *queries] + ([] if before is None else [before])
    return pl.pallas_call(
        functools.partial(near_kernel, flips),
        out_shape=jax.ShapeDtypeStruct((SUPER, DH), jnp.float32),
        in_specs=[pl.BlockSpec(memory_space=pltpu.SMEM)] + [whole()] * (len(args) - 1),
        out_specs=whole(),
        compiler_params=pltpu.CompilerParams(vmem_limit_bytes=VMEM),
        cost_estimate=pl.CostEstimate(flops=1, bytes_accessed=1, transcendentals=0),
        name="near_%d" % flips[0],
    )(*args)


def key_grad_kernel(part_ref, near_ref, out_ref):
    total = near_ref[...]
    for z in range(4):
        total = total + part_ref[z].astype(jnp.float32)
    grad = (total * SCALE).T.astype(jnp.bfloat16)
    for core in range(2):
        rows = [x * 32 + core * 16 for x in range(4)]
        piece = jnp.concatenate([grad[r:r + 16] for r in rows], axis=0)
        for j in range(4):
            out_ref[core, j] = piece


def key_grad_call(parts, near):
    return pl.pallas_call(
        key_grad_kernel,
        out_shape=jax.ShapeDtypeStruct((2, 4, 64, SUPER), jnp.bfloat16),
        in_specs=[whole()] * 2,
        out_specs=whole(),
        compiler_params=pltpu.CompilerParams(vmem_limit_bytes=VMEM),
        name="key_grad",
    )(parts, near)


def project_kernel(core_ref, grad_ref, *refs):
    out_ref = refs[-1]
    total = None
    for flip, x_ref in enumerate(refs[:-1]):
        grad = grad_ref[core_ref[0] ^ flip].reshape(256, SUPER)
        x = x_ref[...].reshape(SUPER, D // 4)
        term = lax.dot_general(grad, x, NN, preferred_element_type=jnp.float32)
        total = term if total is None else total + term
    total = total.astype(jnp.bfloat16)
    for c in range(16):
        for z in range(4):
            out_ref[c, z] = total[c * 16:(c + 1) * 16, z * 256:(z + 1) * 256]


def project(core, grads, features):
    return pl.pallas_call(
        project_kernel,
        out_shape=jax.ShapeDtypeStruct((16, 4, 16, 256), jnp.bfloat16),
        in_specs=[pl.BlockSpec(memory_space=pltpu.SMEM)] + [whole()] * 3,
        out_specs=whole(),
        compiler_params=pltpu.CompilerParams(vmem_limit_bytes=VMEM),
        name="project",
    )(core, grads, *features)


def total_kernel(part_ref, out_ref):
    def step(i, total):
        return total + part_ref[i].astype(jnp.float32)

    total = part_ref[0].astype(jnp.float32)
    for i in range(1, 64):
        total = step(i, total)
    out_ref[...] = total


def total_call(parts):
    return pl.pallas_call(
        total_kernel,
        out_shape=jax.ShapeDtypeStruct((16, 256), jnp.float32),
        in_specs=[whole()],
        out_specs=whole(),
        compiler_params=pltpu.CompilerParams(vmem_limit_bytes=VMEM),
        name="total",
    )(parts)


def body(query, grad_out, keys, values, log_norm, row_dots, block_input, route_index, counts):
    del route_index
    zh = lax.axis_index("zh").astype(jnp.int32)
    home = lax.axis_index(HOME).astype(jnp.int32)
    core = lax.axis_index("core").astype(jnp.int32)
    kv = pack_kv(counts, keys[0], values[0]).reshape(16, 2, CAP, DH)
    kv = lax.all_to_all(kv, ("zh",) + HOME, 0, 0)
    norms_t, dots_t = log_norm[0].T, row_dots[0].T

    def to_home(x, flip):
        if flip == 0:
            return x
        return lax.ppermute(x, HOME, [(i, i ^ flip) for i in range(4)])

    def queries(flip):
        head = (home ^ flip).reshape(1)
        return to_home(pack_q(head, counts, query[0], grad_out[0], norms_t, dots_t), flip)

    place = jnp.stack([zh, home])
    own, beside_y, beside_z, diagonal = (queries(flip) for flip in range(4))
    pieces = list(pack_x(home.reshape(1), counts, block_input[0]))
    pieces[1] = to_home(pieces[1], 1)
    kv, beside_y = lax.optimization_barrier((kv, beside_y))
    far = far_call(place, kv, [own, beside_y])
    near = near_call(place, kv, (0, 1), [own, beside_y])
    far, near, *pieces[2:] = lax.optimization_barrier((far, near, *pieces[2:]))
    pieces[2:] = to_home(pieces[2], 2), to_home(pieces[3], 3)
    far, near, beside_z, diagonal = lax.optimization_barrier((far, near, beside_z, diagonal))
    far = far_call(place, kv, [beside_z, diagonal], far, jnp.bfloat16)
    far, *pieces = lax.optimization_barrier((far, *pieces))
    parts = lax.all_to_all(far, "zh", 0, 0)
    mine = join_x(home.reshape(1), pieces)
    other = lax.ppermute(mine, "core", [(0, 1), (1, 0)])
    near = near_call(place, kv, (2, 3), [beside_z, diagonal], near)
    grads = key_grad_call(parts, near)
    grads = lax.all_to_all(grads.reshape(8, 64, SUPER), ("core",) + HOME, 0, 0)
    local = project(core.reshape(1), grads.reshape(2, 4, 64, SUPER), [mine, other])
    parts = lax.all_to_all(local.reshape(64, 16, 256), ("yh", "x", "zh"), 0, 0)
    return total_call(parts).T


def solution(mesh):
    fine = Mesh(
        np.asarray(mesh.devices).reshape(4, 4, 2, 4, 2, 2), ("yh", "x", "core", "zh", "zl", "yl")
    )
    dp, ctx = ("yh", "x", "core"), ("zh", "zl", "yl")
    in_specs = (P(dp, ctx, None),) * 7 + (P(dp, ctx),) * 2
    return jax.shard_map(body, mesh=fine, in_specs=in_specs, out_specs=P(ctx, dp), check_vma=False)
```
